32 devices in a mesh: groups: 2 (over x), sect: 2 (over core), tile: 8 (over z, y).
Axes of the slice: x: 2, y: 2, z: 4, core: 2. Of those that a mesh axis runs over, the one named last changes fastest.
Arguments:
- features: bfloat16 [4, 16, 64, 512], P(('groups', 'sect'), 'tile'), parts along dimension 0, may hold values from -6 to 6
- conv_first: bfloat16 [3, 3, 3, 512, 512], replicated, may hold values from -0.0546875 to 0.0546875
- bias_first: bfloat16 [512], replicated, may hold values from -3 to 3
- conv_second: bfloat16 [3, 3, 3, 512, 256], replicated, may hold values from -0.0546875 to 0.0546875
- bias_second: bfloat16 [256], replicated, may hold values from -3 to 3
- conv_third: bfloat16 [3, 3, 3, 256, 128], replicated, may hold values from -0.078125 to 0.078125
- bias_third: bfloat16 [128], replicated, may hold values from -3 to 3
Outputs:
- decoded: bfloat16 [4, 64, 256, 128], P(('groups', 'sect'), 'tile'), parts along dimension 0
The draws below stay inside these ranges and needn't reach their ends.
There are 2 independent parts, one for each index of `groups`. The reference program is written for one: setup_inputs(seed, part) draws one part's arguments, and reference() takes and returns one part's arrays. A program takes and returns all parts, laid end to end along the dimension named above; an argument that names none is the same for every part. Nothing has to cross between parts.
All inputs are finite; a program needn't handle non-finite values.
Results may differ from the reference program's by a relative error of at most 0.014.
Values may be sent and summed in bfloat16 or wider, within the bound.
A program may use at most 128 MiB of HBM per device.

```python
import jax
import jax.numpy as jnp

C1 = 512
C2 = 256
C3 = 128
WA = 64
FRAMES = 2
HA = 16


def block_scale(rng, extent, shards, smallest, high):
    def one(axis_at, shards_of):
        draws = jax.random.uniform(jax.random.fold_in(jax.random.fold_in(rng, 6), axis_at), (shards_of,), jnp.float32, smallest / len(shards), high / len(shards))
        return jnp.repeat(jnp.exp(draws), extent[axis_at] // shards_of).reshape((-1,) + (1,) * (len(extent) - axis_at - 1))

    gain = one(*shards[0])
    for cut in shards[1:]:
        gain = gain * one(*cut)
    return gain


def bell_draw(rng, shape, width, reach, shards=(), dtype=jnp.bfloat16):
    level = block_scale(rng, shape, shards, -0.22, 0.18) if shards else 1.0
    result = jax.random.normal(rng, shape, jnp.float32) * width * level
    return jnp.minimum(jnp.maximum(result, -reach), reach).astype(dtype)


def setup_inputs(seed: int = 0, part: int = 0) -> dict:
    streams_of = jax.random.split(jax.random.key(seed), 8)
    own_keys = jax.random.split(jax.random.fold_in(streams_of[7], part), 8)
    return {
        "features": bell_draw(own_keys[0], (FRAMES, HA, WA, C1), 1.0, 6.0, ((0, 2), (1, 8))),
        "conv_first": bell_draw(streams_of[1], (3, 3, 3, C1, C1), (27 * C1) ** -0.5, 0.0546875),
        "bias_first": bell_draw(streams_of[2], (C1,), 0.5, 3.0),
        "conv_second": bell_draw(streams_of[3], (3, 3, 3, C1, C2), (27 * C1) ** -0.5, 0.0546875),
        "bias_second": bell_draw(streams_of[4], (C2,), 0.5, 3.0),
        "conv_third": bell_draw(streams_of[5], (3, 3, 3, C2, C3), (27 * C2) ** -0.5, 0.078125),
        "bias_third": bell_draw(streams_of[6], (C3,), 0.5, 3.0),
    }


def widen(padded, upsample):
    if upsample:
        padded = jnp.repeat(jnp.repeat(padded, 2, axis=0), 2, axis=1)[1:-1]
    return jnp.pad(padded, ((0, 0), (1, 1), (0, 0)))


def apply_taps(cur_pad, prev_pad, weight, offset):
    row_count = cur_pad.shape[0] - 2
    col_count = cur_pad.shape[1] - 2
    chan_count = cur_pad.shape[2]
    summed = jnp.zeros((row_count * col_count, weight.shape[4]), jnp.float32)
    for row_tap in range(3):
        for col_tap in range(3):
            cur_win = cur_pad[row_tap:row_tap + row_count, col_tap:col_tap + col_count].reshape(row_count * col_count, chan_count)
            prev_win = prev_pad[row_tap:row_tap + row_count, col_tap:col_tap + col_count].reshape(row_count * col_count, chan_count)
            summed = summed + (jnp.dot(prev_win, weight[0, row_tap, col_tap], preferred_element_type=jnp.float32)
                               + jnp.dot(prev_win, weight[1, row_tap, col_tap], preferred_element_type=jnp.float32)
                               + jnp.dot(cur_win, weight[2, row_tap, col_tap], preferred_element_type=jnp.float32))
    return summed.reshape(row_count, col_count, -1) + offset.astype(jnp.float32)


def causal(active, weight, offset, upsample):
    earlier = widen(jnp.pad(active[0], ((1, 1), (0, 0), (0, 0))), upsample)
    later = widen(jnp.pad(active[1], ((1, 1), (0, 0), (0, 0))), upsample)
    return jnp.stack([apply_taps(earlier, earlier, weight, offset), apply_taps(later, earlier, weight, offset)])


def reference(features, conv_first, bias_first, conv_second, bias_second, conv_third, bias_third):
    silu_in = jax.nn.silu(features.astype(jnp.float32)).astype(jnp.bfloat16)
    hidden = (features.astype(jnp.float32) + causal(silu_in, conv_first, bias_first, False)).astype(jnp.bfloat16)
    silu_mid = jax.nn.silu(hidden.astype(jnp.float32)).astype(jnp.bfloat16)
    silu_low = jax.nn.silu(causal(silu_mid, conv_second, bias_second, True)).astype(jnp.bfloat16)
    return causal(silu_low, conv_third, bias_third, True).astype(jnp.bfloat16)
```

```python
import functools

import jax
import jax.numpy as jnp
from jax import lax
from jax.experimental import pallas as pl
from jax.experimental.pallas import tpu as pltpu
from jax.sharding import PartitionSpec as P

MESH = pl.DeviceIdType.MESH
F32 = jnp.float32
BF16 = jnp.bfloat16


def silu(v):
    return v / (1.0 + jnp.exp(-v))


def merge_upsampled(read, write):
    taps = [[read(i, j) for j in range(3)] for i in range(3)]
    for p in range(2):
        for q in range(2):
            if p == 0:
                row = taps[0] if q == 0 else [taps[1][j] + taps[2][j] for j in range(3)]
            else:
                row = [taps[0][j] + taps[1][j] for j in range(3)] if q == 0 else taps[2]
            write(p, q, 0, 0, row[1] + row[2])
            write(p, q, 0, 1, row[0] + row[1])
            write(p, q, 1, 0, row[0])
            write(p, q, 1, 1, row[2])


def kernel(
    count, feat, w1h, b1, w2h, b2, w3h, b3, out,
    fbuf, sbuf, w1, w2, w3, m2, m3, mid, low, acc2, acc3, stage, obuf,
    w_sem, own_sem, out_sem, nb_send, nb_recv, fw_send, fw_recv, mid_send, mid_recv, low_send, low_recv,
):
    s = lax.axis_index("sect")
    t = lax.axis_index("tile")
    rows, cols, c1 = feat.shape[1], feat.shape[2], feat.shape[3]
    c2, c3 = w2h.shape[4], w3h.shape[4]
    h1, h2 = c1 // 2, c2 // 2
    total = rows + 4
    has_up, has_down = t > 0, t < count - 1
    up, down = lax.rem(t + count - 1, count), lax.rem(t + 1, count)
    sib = {"sect": 1 - s}

    own = pltpu.make_async_copy(feat.at[0], fbuf.at[s, pl.ds(2, rows)], own_sem)
    own.start()
    o1 = pl.multiple_of(s * h1, h1)
    o2 = pl.multiple_of(s * h2, h2)
    halves1 = [o1, pl.multiple_of((1 - s) * h1, h1)]
    halves2 = [o2, pl.multiple_of((1 - s) * h2, h2)]
    load1 = [
        pltpu.make_async_copy(w1h.at[:, :, j, :, pl.ds(o1, h1)], w1.at[:, :, j], w_sem.at[j])
        for j in range(3)
    ]
    load2 = [
        pltpu.make_async_copy(
            w2h.at[:, :, :, pl.ds(halves1[k], h1), pl.ds(o2, h2)], w2.at[k], w_sem.at[3 + k]
        )
        for k in range(2)
    ]
    load3 = [
        pltpu.make_async_copy(w3h.at[:, :, :, pl.ds(halves2[k], h2), :], w3.at[k], w_sem.at[5 + k])
        for k in range(2)
    ]
    for load in load1 + load2 + load3:
        load.start()

    barrier = pltpu.get_barrier_semaphore()
    pl.semaphore_signal(barrier, inc=1, device_id=sib, device_id_type=MESH)

    @pl.when(has_up)
    def _():
        pl.semaphore_signal(barrier, inc=1, device_id={"tile": up}, device_id_type=MESH)

    @pl.when(has_down)
    def _():
        pl.semaphore_signal(barrier, inc=1, device_id={"tile": down}, device_id_type=MESH)

    pl.semaphore_wait(barrier, 1 + has_up.astype(jnp.int32) + has_down.astype(jnp.int32))

    def remote(src, dst, send, recv, device):
        return pltpu.make_async_remote_copy(
            src_ref=src, dst_ref=dst, send_sem=send, recv_sem=recv, device_id=device, device_id_type=MESH
        )

    plan = [
        (rows - 1, 1, down, has_down, has_up),
        (0, rows + 2, up, has_up, has_down),
        (rows - 2, 0, down, has_down, has_up),
        (1, rows + 3, up, has_up, has_down),
    ]
    direct = [
        remote(feat.at[0, src], fbuf.at[s, dst], nb_send.at[n], nb_recv.at[n], {"tile": to})
        for n, (src, dst, to, _, _) in enumerate(plan)
    ]
    forward = [
        remote(fbuf.at[s, dst], fbuf.at[s, dst], fw_send.at[n], fw_recv.at[n], sib)
        for n, (_, dst, _, _, _) in enumerate(plan)
    ]
    swap = remote(feat.at[0], fbuf.at[s, pl.ds(2, rows)], fw_send.at[4], fw_recv.at[4], sib)
    for n in range(4):
        pl.when(plan[n][3])(direct[n].start)
    swap.start()

    def silu_rows(frame, row, size):
        sbuf[frame, pl.ds(row * cols, size * cols), :] = silu(
            fbuf[frame, pl.ds(row, size)].astype(F32)
        ).astype(BF16).reshape(size * cols, c1)

    for n in range(4):
        dst = plan[n][1]

        @pl.when(jnp.logical_not(plan[n][4]))
        def _(dst=dst):
            for f in range(2):
                fbuf[f, dst] = jnp.zeros((cols, c1), BF16)

    def early1(j):
        load1[j].wait()
        for i in range(3):
            w1[0, i, j] = w1[0, i, j] + w1[1, i, j]

    def pass_on(n):
        @pl.when(plan[n][4])
        def _():
            direct[n].wait_recv()
            forward[n].start()

    def arrived(n):
        @pl.when(plan[n][4])
        def _():
            forward[n].wait_recv()
        for f in range(2):
            silu_rows(f, plan[n][1], 1)

    early1(0)
    early1(1)
    early1(2)
    own.wait()
    swap.wait_recv()
    for f in range(2):
        silu_rows(f, 2, rows)
    pass_on(0)
    pass_on(1)

    def merge(buf, wide, half, c, size):
        def read(i, j):
            if c == 0:
                return buf[half, 0, i, j] + buf[half, 1, i, j]
            return buf[half, 2, i, j]

        def write(p, q, outer, phase, value):
            n = value.shape[1]
            wide[c, half, p, outer, pl.ds(q * size, size), pl.ds(phase * n, n)] = value

        merge_upsampled(read, write)

    for k in range(2):
        load2[k].wait()
        for c in range(2):
            merge(w2, m2, k, c, h1)
    for k in range(2):
        load3[k].wait()
        for c in range(2):
            merge(w3, m3, k, c, h2)

    def shifts(value):
        size = value.shape[0]
        place = lax.rem(lax.broadcasted_iota(jnp.int32, value.shape, 0), cols)

        def later():
            return jnp.where(place == 0, 0.0, pltpu.roll(value, 1, 0))

        def sooner():
            return jnp.where(place == cols - 1, 0.0, pltpu.roll(value, size - 1, 0))

        return later, sooner

    bias1 = b1[:, pl.ds(o1, h1)].astype(F32)
    bias2 = b2[:, pl.ds(o2, h2)].astype(F32)
    bias3 = b3[...].astype(F32)

    def first(hidden_rows):
        def gather(frames):
            return jnp.concatenate(
                [
                    jnp.concatenate(
                        [
                            sbuf[f, pl.ds((start + i) * cols, size * cols), :]
                            for i in range(3)
                        ],
                        axis=1,
                    )
                    for f in frames
                    for start, size in hidden_rows
                ],
                axis=0,
            )

        height = sum(size for _, size in hidden_rows) * cols
        both, earlier = gather((0, 1)), gather((0,))
        result = []
        summed = [None, None]
        for j in (1, 0, 2):
            kernel_now = w1[2, :, j].reshape(3 * c1, h1)
            kernel_early = w1[0, :, j].reshape(3 * c1, h1)
            now = jnp.dot(both, kernel_now, preferred_element_type=F32)
            early = jnp.dot(earlier, kernel_early, preferred_element_type=F32)
            for f in range(2):
                part = now[f * height : (f + 1) * height] + early
                if j == 1:
                    summed[f] = part
                else:
                    later, sooner = shifts(part)
                    summed[f] = summed[f] + (later() if j == 0 else sooner())
        for f in range(2):
            at = 0
            for start, size in hidden_rows:
                for row in range(start, start + size):
                    base = fbuf[f, row + 1, :, pl.ds(o1, h1)].astype(F32)
                    hidden = (base + (summed[f][at : at + cols] + bias1)).astype(BF16).astype(F32)
                    value = silu(hidden)
                    if row == 0:
                        value = jnp.where(has_up, value, 0.0)
                    if row == rows + 1:
                        value = jnp.where(has_down, value, 0.0)
                    mid[0, f, row] = value.astype(BF16)
                    at += cols

    arrived(0)
    arrived(1)
    first([(1, rows)])
    send_mid = [
        remote(mid.at[0, :, pl.ds(1, rows)], mid.at[1, :, pl.ds(1, rows)], mid_send.at[0], mid_recv.at[0], sib),
        remote(mid.at[0, :, 0], mid.at[1, :, 0], mid_send.at[1], mid_recv.at[1], sib),
        remote(mid.at[0, :, rows + 1], mid.at[1, :, rows + 1], mid_send.at[2], mid_recv.at[2], sib),
    ]
    send_mid[0].start()
    pass_on(2)
    pass_on(3)
    arrived(2)
    arrived(3)
    first([(0, 1), (rows + 1, 1)])
    send_mid[1].start()
    send_mid[2].start()

    lines = (rows + 1) * cols

    def second(half, then):
        def gather(f):
            return jnp.concatenate(
                [mid[half, f, pl.ds(q, rows + 1)].reshape(lines, h1) for q in range(2)], axis=1
            )

        earlier = gather(0)
        both = jnp.concatenate([earlier, gather(1)], axis=0)
        for p in range(2):
            for outer in range(2):
                now = jnp.dot(both, m2[1, half, p, outer], preferred_element_type=F32)
                early = jnp.dot(earlier, m2[0, half, p, outer], preferred_element_type=F32)
                for f in range(2):
                    then(p, outer, f, now[f * lines : (f + 1) * lines] + early)

    def keep(p, outer, f, value):
        acc2[p, outer, f] = value

    def add(p, outer, f, value):
        acc2[p, outer, f] = acc2[p, outer, f] + value

    second(0, keep)
    for copy in send_mid:
        copy.wait_recv()
    second(1, add)

    send_low = [
        remote(low.at[0, f], low.at[1, f], low_send.at[f], low_recv.at[f], sib) for f in range(2)
    ]
    last = 2 * rows + 1
    for f in range(2):
        for p in range(2):
            inner, outer = acc2[p, 0, f], acc2[p, 1, f]
            values = [
                inner[:, :h2] + shifts(outer[:, :h2])[0](),
                inner[:, h2:] + shifts(outer[:, h2:])[1](),
            ]
            for phase in range(2):
                value = silu(values[phase] + bias2)
                for m in range(rows + 1):
                    row = 2 * m + 1 - p
                    part = value[m * cols : (m + 1) * cols]
                    if row == 0:
                        part = jnp.where(has_up, part, 0.0)
                    if row == last:
                        part = jnp.where(has_down, part, 0.0)
                    low[0, f, phase, row] = part.astype(BF16)
        if f == 0:
            send_low[0].start()
        else:
            pl.when(s == 0)(send_low[1].start)

    deep = 2 * rows * cols

    def third(half, p, phase):
        x = jnp.concatenate(
            [
                low[half, f, phase, pl.ds(p + q, 2 * rows)].reshape(deep, h2)
                for f in (0, s)
                for q in range(2)
            ],
            axis=1,
        )
        return [
            jnp.dot(
                x,
                jnp.concatenate([m3[0, half, p, outer], m3[1, half, p, outer]], axis=0),
                preferred_element_type=F32,
            )
            for outer in range(2)
        ]

    for p in range(2):
        for phase in range(2):
            for outer, value in enumerate(third(0, p, phase)):
                acc3[p, phase, outer] = value
    send_low[0].wait_recv()
    pl.when(s == 1)(send_low[1].wait_recv)
    put = []
    for p in range(2):
        inner, outer = [], []
        for phase in range(2):
            a, b = third(1, p, phase)
            inner.append(acc3[p, phase, 0] + a)
            outer.append(acc3[p, phase, 1] + b)
        values = [
            inner[0][:, :c3] + shifts(outer[1][:, :c3])[0](),
            inner[0][:, c3:] + outer[1][:, c3:],
            inner[1][:, :c3] + outer[0][:, :c3],
            inner[1][:, c3:] + shifts(outer[0][:, c3:])[1](),
        ]
        for n in range(4):
            for m in range(2 * rows):
                stage[p, m, pl.ds(n, cols, stride=4), :] = values[n][m * cols : (m + 1) * cols] + bias3
        for m in range(2 * rows):
            row = 2 * m + p
            obuf[row] = stage[p, m].astype(BF16)
    copy = pltpu.make_async_copy(obuf, out.at[0], out_sem)
    copy.start()

    for n in range(4):
        pl.when(plan[n][3])(direct[n].wait_send)
        pl.when(plan[n][4])(forward[n].wait_send)
    swap.wait_send()
    for c in send_mid:
        c.wait_send()
    send_low[0].wait_send()
    pl.when(s == 0)(send_low[1].wait_send)
    copy.wait()


def per_device(features, w1, b1, w2, b2, w3, b3):
    count = lax.axis_size("tile")
    _, rows, cols, c1 = features.shape
    c2, c3 = w2.shape[4], w3.shape[4]
    h1, h2 = c1 // 2, c2 // 2
    anywhere = pl.BlockSpec(memory_space=pl.ANY)
    vmem = pl.BlockSpec(memory_space=pltpu.VMEM)
    dma = pltpu.SemaphoreType.DMA
    return pl.pallas_call(
        functools.partial(kernel, count),
        out_shape=jax.ShapeDtypeStruct((1, 4 * rows, 4 * cols, c3), BF16),
        in_specs=[anywhere, anywhere, vmem, anywhere, vmem, anywhere, vmem],
        out_specs=anywhere,
        scratch_shapes=[
            pltpu.VMEM((2, rows + 4, cols, c1), BF16),
            pltpu.VMEM((2, (rows + 4) * cols, c1), BF16),
            pltpu.VMEM((3, 3, 3, c1, h1), BF16),
            pltpu.VMEM((2, 3, 3, 3, h1, h2), BF16),
            pltpu.VMEM((2, 3, 3, 3, h2, c3), BF16),
            pltpu.VMEM((2, 2, 2, 2, 2 * h1, 2 * h2), BF16),
            pltpu.VMEM((2, 2, 2, 2, 2 * h2, 2 * c3), BF16),
            pltpu.VMEM((2, 2, rows + 2, cols, h1), BF16),
            pltpu.VMEM((2, 2, 2, 2 * rows + 2, cols, h2), BF16),
            pltpu.VMEM((2, 2, 2, (rows + 1) * cols, 2 * h2), F32),
            pltpu.VMEM((2, 2, 2, 2 * rows * cols, 2 * c3), F32),
            pltpu.VMEM((2, 2 * rows, 4 * cols, c3), F32),
            pltpu.VMEM((4 * rows, 4 * cols, c3), BF16),
            dma((7,)),
            dma(()),
            dma(()),
            dma((4,)),
            dma((4,)),
            dma((5,)),
            dma((5,)),
            dma((3,)),
            dma((3,)),
            dma((2,)),
            dma((2,)),
        ],
        compiler_params=pltpu.CompilerParams(
            collective_id=0, has_side_effects=True, vmem_limit_bytes=52 * 2**20
        ),
    )(features, w1, b1.reshape(1, c1), w2, b2.reshape(1, c2), w3, b3.reshape(1, c3))


def solution(mesh):
    return jax.shard_map(
        per_device,
        mesh=mesh,
        in_specs=(P(("groups", "sect"), "tile", None, None), P(), P(), P(), P(), P(), P()),
        out_specs=P(("groups", "sect"), "tile", None, None),
        check_vma=False,
    )
```

```python
import functools

import jax
import jax.numpy as jnp
from jax import lax
from jax.experimental import pallas as pl
from jax.experimental.pallas import tpu as pltpu
from jax.sharding import PartitionSpec as P

MESH = pl.DeviceIdType.MESH
F32 = jnp.float32
BF16 = jnp.bfloat16
PIECES = 2


def silu(v):
    return v / (1.0 + jnp.exp(-v))


def merge_upsampled(read, write):
    taps = [[read(i, j) for j in range(3)] for i in range(3)]
    for p in range(2):
        for q in range(2):
            if p == 0:
                row = taps[0] if q == 0 else [taps[1][j] + taps[2][j] for j in range(3)]
            else:
                row = [taps[0][j] + taps[1][j] for j in range(3)] if q == 0 else taps[2]
            write(p, q, 0, 0, row[1] + row[2])
            write(p, q, 0, 1, row[0] + row[1])
            write(p, q, 1, 0, row[0])
            write(p, q, 1, 1, row[2])


def kernel(
    count, feat, w1h, b1h, w2h, b2h, w3h, b3h, out,
    fbuf, sbuf, b1, b2, b3, w1, w2, w3, m2, m3, mid, low, acc2, acc3, stage,
    w_sem, own_sem, nb_send, nb_recv, fw_send, fw_recv, mid_send, mid_recv, low_send, low_recv,
):
    s = lax.axis_index("sect")
    t = lax.axis_index("tile")
    rows, cols, c1 = feat.shape[1], feat.shape[2], feat.shape[3]
    c2, c3 = w2h.shape[4], w3h.shape[4]
    h1, h2 = c1 // 2, c2 // 2
    assert rows == 2 and count % 2 == 0
    has_up, has_down = t > 0, t < count - 1
    sib = {"sect": 1 - s}

    own = pltpu.make_async_copy(feat.at[0], fbuf.at[s, pl.ds(2, rows)], own_sem)
    own.start()
    o1 = pl.multiple_of(s * h1, h1)
    o2 = pl.multiple_of(s * h2, h2)
    halves1 = [o1, pl.multiple_of((1 - s) * h1, h1)]
    halves2 = [o2, pl.multiple_of((1 - s) * h2, h2)]
    load1 = [
        pltpu.make_async_copy(w1h.at[:, :, j, :, pl.ds(o1, h1)], w1.at[:, :, j], w_sem.at[j])
        for j in range(3)
    ]
    load2 = [
        pltpu.make_async_copy(
            w2h.at[:, :, :, pl.ds(halves1[k], h1), pl.ds(o2, h2)], w2.at[k], w_sem.at[3 + k]
        )
        for k in range(2)
    ]
    load3 = [
        pltpu.make_async_copy(w3h.at[:, :, :, pl.ds(halves2[k], h2), :], w3.at[k], w_sem.at[5 + k])
        for k in range(2)
    ]
    load_b = [
        pltpu.make_async_copy(src, dst, w_sem.at[7 + n])
        for n, (src, dst) in enumerate(((b1h, b1), (b2h, b2), (b3h, b3)))
    ]
    for load in load_b + load1 + load2 + load3:
        load.start()

    barrier = pltpu.get_barrier_semaphore()
    even = lax.rem(t, 2) == 0
    partner = jnp.where(even, t + 1, t - 1)
    has_low, has_high = t >= 2, t + 2 < count
    goes = jnp.where(even, has_high, has_low)
    comes = jnp.where(even, has_low, has_high)
    onward = lax.rem(jnp.where(even, t + 2, t + count - 2), count)
    near_side = jnp.where(even, rows + 2, 0)
    far_side = jnp.where(even, 0, rows + 2)

    def greet(device):
        pl.semaphore_signal(barrier, inc=1, device_id=device, device_id_type=MESH)

    greet(sib)
    greet({"tile": partner})
    pl.when(has_low)(lambda: greet({"tile": lax.rem(t + count - 2, count)}))
    pl.when(has_high)(lambda: greet({"tile": lax.rem(t + 2, count)}))
    pl.semaphore_wait(barrier, 2 + has_low.astype(jnp.int32) + has_high.astype(jnp.int32))

    def remote(src, dst, send, recv, device):
        return pltpu.make_async_remote_copy(
            src_ref=src, dst_ref=dst, send_sem=send, recv_sem=recv, device_id=device, device_id_type=MESH
        )

    piece = cols // PIECES
    chunks = [
        (jnp.where(even, k, 1 - k), pl.ds(h * piece, piece)) for k in range(2) for h in range(PIECES)
    ]
    each = len(chunks)
    theirs = [(1 - row, part) for row, part in chunks]
    pair = [
        remote(feat.at[0, row, part], fbuf.at[s, far_side + row, part], nb_send.at[n], nb_recv.at[n], {"tile": partner})
        for n, (row, part) in enumerate(chunks)
    ]
    relay = [
        remote(
            fbuf.at[s, near_side + row, part], fbuf.at[s, far_side + row, part],
            nb_send.at[each + n], nb_recv.at[each + n], {"tile": onward},
        )
        for n, (row, part) in enumerate(theirs)
    ]
    forward = [
        remote(fbuf.at[s, side + row, part], fbuf.at[s, side + row, part], fw_send.at[n], fw_recv.at[n], sib)
        for n, (side, row, part) in enumerate(
            [(near_side, *c) for c in theirs] + [(far_side, *c) for c in theirs]
        )
    ]
    swap = remote(
        feat.at[0], fbuf.at[s, pl.ds(2, rows)], fw_send.at[2 * each], fw_recv.at[2 * each], sib
    )
    for c in pair:
        c.start()
    swap.start()

    def silu_rows(frame, row, size):
        sbuf[frame, pl.ds(row * cols, size * cols), :] = silu(
            fbuf[frame, pl.ds(row, size)].astype(F32)
        ).astype(BF16).reshape(size * cols, c1)

    @pl.when(jnp.logical_not(comes))
    def _():
        for f in range(2):
            for row in range(2):
                fbuf[f, far_side + row] = jnp.zeros((cols, c1), BF16)

    def early1(j):
        load1[j].wait()
        for i in range(3):
            w1[0, i, j] = w1[0, i, j] + w1[1, i, j]

    def pass_pair(n):
        pair[n].wait_recv()
        pl.when(goes)(relay[n].start)
        forward[n].start()

    def pass_relay(first_one, stop):
        @pl.when(comes)
        def _():
            for n in range(first_one, stop):
                relay[n].wait_recv()
                forward[each + n].start()

    half = each // 2
    for n in range(half):
        pass_pair(n)
    early1(0)
    for n in range(half, each):
        pass_pair(n)
    early1(1)
    early1(2)
    own.wait()
    swap.wait_recv()
    for f in range(2):
        silu_rows(f, 2, rows)
    pass_relay(0, half)

    def merge(buf, wide, half, c, size):
        def read(i, j):
            if c == 0:
                return buf[half, 0, i, j] + buf[half, 1, i, j]
            return buf[half, 2, i, j]

        def write(p, q, outer, phase, value):
            n = value.shape[1]
            wide[c, half, p, outer, pl.ds(q * size, size), pl.ds(phase * n, n)] = value

        merge_upsampled(read, write)

    for k in range(2):
        load2[k].wait()
        for c in range(2):
            merge(w2, m2, k, c, h1)
    for k in range(2):
        load3[k].wait()
        for c in range(2):
            merge(w3, m3, k, c, h2)

    def shifts(value):
        size = value.shape[0]
        place = lax.rem(lax.broadcasted_iota(jnp.int32, value.shape, 0), cols)

        def later():
            return jnp.where(place == 0, 0.0, pltpu.roll(value, 1, 0))

        def sooner():
            return jnp.where(place == cols - 1, 0.0, pltpu.roll(value, size - 1, 0))

        return later, sooner

    for load in load_b:
        load.wait()
    bias1 = b1[...].astype(F32).reshape(1, c1)
    bias1 = jnp.where(s == 0, bias1[:, :h1], bias1[:, h1:])
    bias2 = b2[...].astype(F32).reshape(1, c2)
    bias2 = jnp.where(s == 0, bias2[:, :h2], bias2[:, h2:])
    bias3 = b3[...].astype(F32).reshape(1, c3)

    def first(hidden_rows):
        def gather(frames):
            return jnp.concatenate(
                [
                    jnp.concatenate(
                        [
                            sbuf[f, pl.ds((start + i) * cols, size * cols), :]
                            for i in range(3)
                        ],
                        axis=1,
                    )
                    for f in frames
                    for start, size in hidden_rows
                ],
                axis=0,
            )

        height = sum(size for _, size in hidden_rows) * cols
        both, earlier = gather((0, 1)), gather((0,))
        result = []
        summed = [None, None]
        for j in (1, 0, 2):
            kernel_now = w1[2, :, j].reshape(3 * c1, h1)
            kernel_early = w1[0, :, j].reshape(3 * c1, h1)
            now = jnp.dot(both, kernel_now, preferred_element_type=F32)
            early = jnp.dot(earlier, kernel_early, preferred_element_type=F32)
            for f in range(2):
                part = now[f * height : (f + 1) * height] + early
                if j == 1:
                    summed[f] = part
                else:
                    later, sooner = shifts(part)
                    summed[f] = summed[f] + (later() if j == 0 else sooner())
        for f in range(2):
            at = 0
            for start, size in hidden_rows:
                for row in range(start, start + size):
                    base = fbuf[f, row + 1, :, pl.ds(o1, h1)].astype(F32)
                    hidden = (base + (summed[f][at : at + cols] + bias1)).astype(BF16).astype(F32)
                    value = silu(hidden)
                    if row == 0:
                        value = jnp.where(has_up, value, 0.0)
                    if row == rows + 1:
                        value = jnp.where(has_down, value, 0.0)
                    mid[0, f, row] = value.astype(BF16)
                    at += cols

    pass_relay(half, each)
    for n in range(each):
        forward[n].wait_recv()

    @pl.when(comes)
    def _():
        for n in range(half):
            forward[each + n].wait_recv()

    for f in range(2):
        silu_rows(f, 1, 1)
        silu_rows(f, rows + 2, 1)
    first([(1, rows)])
    send_mid = [
        remote(mid.at[0, :, pl.ds(1, rows)], mid.at[1, :, pl.ds(1, rows)], mid_send.at[0], mid_recv.at[0], sib),
        remote(mid.at[0, :, 0], mid.at[1, :, 0], mid_send.at[1], mid_recv.at[1], sib),
        remote(mid.at[0, :, rows + 1], mid.at[1, :, rows + 1], mid_send.at[2], mid_recv.at[2], sib),
    ]
    send_mid[0].start()

    @pl.when(comes)
    def _():
        for n in range(half, each):
            forward[each + n].wait_recv()

    for f in range(2):
        silu_rows(f, 0, 1)
        silu_rows(f, rows + 3, 1)
    first([(0, 1), (rows + 1, 1)])
    send_mid[1].start()
    send_mid[2].start()

    lines = (rows + 1) * cols

    def second(half, then):
        def gather(f):
            return jnp.concatenate(
                [mid[half, f, pl.ds(q, rows + 1)].reshape(lines, h1) for q in range(2)], axis=1
            )

        earlier = gather(0)
        both = jnp.concatenate([earlier, gather(1)], axis=0)
        for p in range(2):
            for outer in range(2):
                now = jnp.dot(both, m2[1, half, p, outer], preferred_element_type=F32)
                early = jnp.dot(earlier, m2[0, half, p, outer], preferred_element_type=F32)
                for f in range(2):
                    then(p, outer, f, now[f * lines : (f + 1) * lines] + early)

    def keep(p, outer, f, value):
        acc2[p, outer, f] = value

    def add(p, outer, f, value):
        acc2[p, outer, f] = acc2[p, outer, f] + value

    second(0, keep)
    for copy in send_mid:
        copy.wait_recv()
    second(1, add)

    send_low = [
        remote(low.at[0, f], low.at[1, f], low_send.at[f], low_recv.at[f], sib) for f in range(2)
    ]
    last = 2 * rows + 1
    for f in range(2):
        for p in range(2):
            inner, outer = acc2[p, 0, f], acc2[p, 1, f]
            values = [
                inner[:, :h2] + shifts(outer[:, :h2])[0](),
                inner[:, h2:] + shifts(outer[:, h2:])[1](),
            ]
            for phase in range(2):
                value = silu(values[phase] + bias2)
                for m in range(rows + 1):
                    row = 2 * m + 1 - p
                    part = value[m * cols : (m + 1) * cols]
                    if row == 0:
                        part = jnp.where(has_up, part, 0.0)
                    if row == last:
                        part = jnp.where(has_down, part, 0.0)
                    low[0, f, phase, row] = part.astype(BF16)
        if f == 0:
            send_low[0].start()
        else:
            pl.when(s == 0)(send_low[1].start)

    deep = 2 * rows * cols

    def third(half, p, phase):
        x = jnp.concatenate(
            [
                low[half, f, phase, pl.ds(p + q, 2 * rows)].reshape(deep, h2)
                for f in (0, s)
                for q in range(2)
            ],
            axis=1,
        )
        return [
            jnp.dot(
                x,
                jnp.concatenate([m3[0, half, p, outer], m3[1, half, p, outer]], axis=0),
                preferred_element_type=F32,
            )
            for outer in range(2)
        ]

    for p in range(2):
        for phase in range(2):
            for outer, value in enumerate(third(0, p, phase)):
                acc3[p, phase, outer] = value
    send_low[0].wait_recv()
    pl.when(s == 1)(send_low[1].wait_recv)
    for p in range(2):
        inner, outer = [], []
        for phase in range(2):
            a, b = third(1, p, phase)
            inner.append(acc3[p, phase, 0] + a)
            outer.append(acc3[p, phase, 1] + b)
        values = [
            inner[0][:, :c3] + shifts(outer[1][:, :c3])[0](),
            inner[0][:, c3:] + outer[1][:, c3:],
            inner[1][:, :c3] + outer[0][:, :c3],
            inner[1][:, c3:] + shifts(outer[0][:, c3:])[1](),
        ]
        for n in range(4):
            for m in range(2 * rows):
                stage[p, m, pl.ds(n, cols, stride=4), :] = values[n][m * cols : (m + 1) * cols] + bias3
        for m in range(2 * rows):
            row = 2 * m + p
            out[0, row] = stage[p, m].astype(BF16)

    for n in range(each):
        pair[n].wait_send()
        forward[n].wait_send()
        pl.when(goes)(relay[n].wait_send)
        pl.when(comes)(forward[each + n].wait_send)
    swap.wait_send()
    for c in send_mid:
        c.wait_send()
    send_low[0].wait_send()
    pl.when(s == 0)(send_low[1].wait_send)


def per_device(features, w1, b1, w2, b2, w3, b3):
    count = lax.axis_size("tile")
    _, rows, cols, c1 = features.shape
    c2, c3 = w2.shape[4], w3.shape[4]
    h1, h2 = c1 // 2, c2 // 2
    anywhere = pl.BlockSpec(memory_space=pltpu.HBM)
    vmem = pl.BlockSpec(memory_space=pltpu.VMEM)
    dma = pltpu.SemaphoreType.DMA
    features, b1, b2, b3 = [
        pltpu.with_memory_space_constraint(x, pltpu.HBM) for x in (features, b1, b2, b3)
    ]
    return pl.pallas_call(
        functools.partial(kernel, count),
        out_shape=jax.ShapeDtypeStruct((1, 4 * rows, 4 * cols, c3), BF16),
        in_specs=[anywhere] * 7,
        out_specs=vmem,
        scratch_shapes=[
            pltpu.VMEM((2, rows + 4, cols, c1), BF16),
            pltpu.VMEM((2, (rows + 4) * cols, c1), BF16),
            pltpu.VMEM((c1,), BF16),
            pltpu.VMEM((c2,), BF16),
            pltpu.VMEM((c3,), BF16),
            pltpu.VMEM((3, 3, 3, c1, h1), BF16),
            pltpu.VMEM((2, 3, 3, 3, h1, h2), BF16),
            pltpu.VMEM((2, 3, 3, 3, h2, c3), BF16),
            pltpu.VMEM((2, 2, 2, 2, 2 * h1, 2 * h2), BF16),
            pltpu.VMEM((2, 2, 2, 2, 2 * h2, 2 * c3), BF16),
            pltpu.VMEM((2, 2, rows + 2, cols, h1), BF16),
            pltpu.VMEM((2, 2, 2, 2 * rows + 2, cols, h2), BF16),
            pltpu.VMEM((2, 2, 2, (rows + 1) * cols, 2 * h2), F32),
            pltpu.VMEM((2, 2, 2, 2 * rows * cols, 2 * c3), F32),
            pltpu.VMEM((2, 2 * rows, 4 * cols, c3), F32),
            dma((10,)),
            dma(()),
            dma((4 * PIECES,)),
            dma((4 * PIECES,)),
            dma((4 * PIECES + 1,)),
            dma((4 * PIECES + 1,)),
            dma((3,)),
            dma((3,)),
            dma((2,)),
            dma((2,)),
        ],
        compiler_params=pltpu.CompilerParams(
            collective_id=0, has_side_effects=True, vmem_limit_bytes=52 * 2**20
        ),
    )(features, w1, b1, w2, b2, w3, b3)


def solution(mesh):
    return jax.shard_map(
        per_device,
        mesh=mesh,
        in_specs=(P(("groups", "sect"), "tile", None, None), P(), P(), P(), P(), P(), P()),
        out_specs=P(("groups", "sect"), "tile", None, None),
        check_vma=False,
    )
```

```python
import functools

import jax
import jax.numpy as jnp
from jax import lax
from jax.experimental import pallas as pl
from jax.experimental.pallas import tpu as pltpu
from jax.sharding import PartitionSpec as P

MESH = pl.DeviceIdType.MESH
F32 = jnp.float32
BF16 = jnp.bfloat16
PIECES = 2


def silu(v):
    return v / (1.0 + jnp.exp(-v))


def merge_upsampled(read, write):
    taps = [[read(i, j) for j in range(3)] for i in range(3)]
    for p in range(2):
        for q in range(2):
            if p == 0:
                row = taps[0] if q == 0 else [taps[1][j] + taps[2][j] for j in range(3)]
            else:
                row = [taps[0][j] + taps[1][j] for j in range(3)] if q == 0 else taps[2]
            write(p, q, 0, 0, row[1] + row[2])
            write(p, q, 0, 1, row[0] + row[1])
            write(p, q, 1, 0, row[0])
            write(p, q, 1, 1, row[2])


def kernel(
    count, feat, w1h, b1h, w2h, b2h, w3h, b3h, out,
    fbuf, sbuf, b1, b2, b3, w1, w2, w3, m2, m3, mid, low, acc2, acc3, stage,
    w_sem, own_sem, nb_send, nb_recv, fw_send, fw_recv, mid_send, mid_recv, low_send, low_recv,
):
    s = lax.axis_index("sect")
    t = lax.axis_index("tile")
    rows, cols, c1 = feat.shape[1], feat.shape[2], feat.shape[3]
    c2, c3 = w2h.shape[4], w3h.shape[4]
    h1, h2 = c1 // 2, c2 // 2
    assert rows == 2 and count % 2 == 0
    has_up, has_down = t > 0, t < count - 1
    sib = {"sect": 1 - s}

    own = pltpu.make_async_copy(feat.at[0], fbuf.at[s, pl.ds(2, rows)], own_sem)
    own.start()
    o1 = pl.multiple_of(s * h1, h1)
    o2 = pl.multiple_of(s * h2, h2)
    halves1 = [o1, pl.multiple_of((1 - s) * h1, h1)]
    halves2 = [o2, pl.multiple_of((1 - s) * h2, h2)]
    load1 = [
        pltpu.make_async_copy(w1h.at[:, :, j, :, pl.ds(o1, h1)], w1.at[:, :, j], w_sem.at[j])
        for j in range(3)
    ]
    load2 = [
        pltpu.make_async_copy(
            w2h.at[:, :, :, pl.ds(halves1[k], h1), pl.ds(o2, h2)], w2.at[k], w_sem.at[3 + k]
        )
        for k in range(2)
    ]
    load3 = [
        pltpu.make_async_copy(w3h.at[:, :, :, pl.ds(halves2[k], h2), :], w3.at[k], w_sem.at[5 + k])
        for k in range(2)
    ]
    load_b = [
        pltpu.make_async_copy(src, dst, w_sem.at[7 + n])
        for n, (src, dst) in enumerate(((b1h, b1), (b2h, b2), (b3h, b3)))
    ]
    for load in load_b + load1:
        load.start()

    barrier = pltpu.get_barrier_semaphore()
    even = lax.rem(t, 2) == 0
    partner = jnp.where(even, t + 1, t - 1)
    has_low, has_high = t >= 2, t + 2 < count
    goes = jnp.where(even, has_high, has_low)
    comes = jnp.where(even, has_low, has_high)
    onward = lax.rem(jnp.where(even, t + 2, t + count - 2), count)
    near_side = jnp.where(even, rows + 2, 0)
    far_side = jnp.where(even, 0, rows + 2)

    def greet(device):
        pl.semaphore_signal(barrier, inc=1, device_id=device, device_id_type=MESH)

    greet(sib)
    greet({"tile": partner})
    pl.when(has_low)(lambda: greet({"tile": lax.rem(t + count - 2, count)}))
    pl.when(has_high)(lambda: greet({"tile": lax.rem(t + 2, count)}))
    pl.semaphore_wait(barrier, 2 + has_low.astype(jnp.int32) + has_high.astype(jnp.int32))

    def remote(src, dst, send, recv, device):
        return pltpu.make_async_remote_copy(
            src_ref=src, dst_ref=dst, send_sem=send, recv_sem=recv, device_id=device, device_id_type=MESH
        )

    piece = cols // PIECES
    chunks = [
        (jnp.where(even, k, 1 - k), pl.ds(h * piece, piece)) for k in range(2) for h in range(PIECES)
    ]
    each = len(chunks)
    theirs = [(1 - row, part) for row, part in chunks]
    pair = [
        remote(feat.at[0, row, part], fbuf.at[s, far_side + row, part], nb_send.at[n], nb_recv.at[n], {"tile": partner})
        for n, (row, part) in enumerate(chunks)
    ]
    relay = [
        remote(
            fbuf.at[s, near_side + row, part], fbuf.at[s, far_side + row, part],
            nb_send.at[each + n], nb_recv.at[each + n], {"tile": onward},
        )
        for n, (row, part) in enumerate(theirs)
    ]
    forward = [
        remote(fbuf.at[s, side + row, part], fbuf.at[s, side + row, part], fw_send.at[n], fw_recv.at[n], sib)
        for n, (side, row, part) in enumerate(
            [(near_side, *c) for c in theirs] + [(far_side, *c) for c in theirs]
        )
    ]
    swap = remote(
        feat.at[0], fbuf.at[s, pl.ds(2, rows)], fw_send.at[2 * each], fw_recv.at[2 * each], sib
    )
    for c in pair:
        c.start()
    swap.start()
    for load in load2 + load3:
        load.start()

    def silu_rows(frame, row, size):
        sbuf[frame, pl.ds(row * cols, size * cols), :] = silu(
            fbuf[frame, pl.ds(row, size)].astype(F32)
        ).astype(BF16).reshape(size * cols, c1)

    @pl.when(jnp.logical_not(comes))
    def _():
        for f in range(2):
            for row in range(2):
                fbuf[f, far_side + row] = jnp.zeros((cols, c1), BF16)

    def early1(j):
        load1[j].wait()
        for i in range(3):
            w1[0, i, j] = w1[0, i, j] + w1[1, i, j]

    def pass_pair(n):
        pair[n].wait_recv()
        pl.when(goes)(relay[n].start)
        forward[n].start()

    def pass_relay(first_one, stop):
        @pl.when(comes)
        def _():
            for n in range(first_one, stop):
                relay[n].wait_recv()
                forward[each + n].start()

    half = each // 2
    for n in range(half):
        pass_pair(n)
    early1(0)
    for n in range(half, each):
        pass_pair(n)
    early1(1)
    early1(2)
    own.wait()
    swap.wait_recv()
    for f in range(2):
        silu_rows(f, 2, rows)
    pass_relay(0, half)

    def merge(buf, wide, half, c, size):
        def read(i, j):
            if c == 0:
                return buf[half, 0, i, j] + buf[half, 1, i, j]
            return buf[half, 2, i, j]

        def write(p, q, outer, phase, value):
            n = value.shape[1]
            wide[c, half, p, outer, pl.ds(q * size, size), pl.ds(phase * n, n)] = value

        merge_upsampled(read, write)

    for k in range(2):
        load2[k].wait()
        for c in range(2):
            merge(w2, m2, k, c, h1)
    for k in range(2):
        load3[k].wait()
        for c in range(2):
            merge(w3, m3, k, c, h2)

    def shifts(value):
        size = value.shape[0]
        place = lax.rem(lax.broadcasted_iota(jnp.int32, value.shape, 0), cols)

        def later():
            return jnp.where(place == 0, 0.0, pltpu.roll(value, 1, 0))

        def sooner():
            return jnp.where(place == cols - 1, 0.0, pltpu.roll(value, size - 1, 0))

        return later, sooner

    for load in load_b:
        load.wait()
    bias1 = b1[...].astype(F32).reshape(1, c1)
    bias1 = jnp.where(s == 0, bias1[:, :h1], bias1[:, h1:])
    bias2 = b2[...].astype(F32).reshape(1, c2)
    bias2 = jnp.where(s == 0, bias2[:, :h2], bias2[:, h2:])
    bias3 = b3[...].astype(F32).reshape(1, c3)

    def first(hidden_rows):
        def gather(frames):
            return jnp.concatenate(
                [
                    jnp.concatenate(
                        [
                            sbuf[f, pl.ds((start + i) * cols, size * cols), :]
                            for i in range(3)
                        ],
                        axis=1,
                    )
                    for f in frames
                    for start, size in hidden_rows
                ],
                axis=0,
            )

        height = sum(size for _, size in hidden_rows) * cols
        both, earlier = gather((0, 1)), gather((0,))
        result = []
        summed = [None, None]
        for j in (1, 0, 2):
            kernel_now = w1[2, :, j].reshape(3 * c1, h1)
            kernel_early = w1[0, :, j].reshape(3 * c1, h1)
            now = jnp.dot(both, kernel_now, preferred_element_type=F32)
            early = jnp.dot(earlier, kernel_early, preferred_element_type=F32)
            for f in range(2):
                part = now[f * height : (f + 1) * height] + early
                if j == 1:
                    summed[f] = part
                else:
                    later, sooner = shifts(part)
                    summed[f] = summed[f] + (later() if j == 0 else sooner())
        for f in range(2):
            at = 0
            for start, size in hidden_rows:
                for row in range(start, start + size):
                    base = fbuf[f, row + 1, :, pl.ds(o1, h1)].astype(F32)
                    hidden = (base + (summed[f][at : at + cols] + bias1)).astype(BF16).astype(F32)
                    value = silu(hidden)
                    if row == 0:
                        value = jnp.where(has_up, value, 0.0)
                    if row == rows + 1:
                        value = jnp.where(has_down, value, 0.0)
                    mid[0, f, row] = value.astype(BF16)
                    at += cols

    pass_relay(half, each)
    for n in range(each):
        forward[n].wait_recv()

    @pl.when(comes)
    def _():
        for n in range(half):
            forward[each + n].wait_recv()

    for f in range(2):
        silu_rows(f, 1, 1)
        silu_rows(f, rows + 2, 1)
    send_mid = [
        remote(mid.at[0, :, pl.ds(1, rows)], mid.at[1, :, pl.ds(1, rows)], mid_send.at[0], mid_recv.at[0], sib),
        remote(mid.at[0, :, 0], mid.at[1, :, 0], mid_send.at[1], mid_recv.at[1], sib),
        remote(mid.at[0, :, rows + 1], mid.at[1, :, rows + 1], mid_send.at[2], mid_recv.at[2], sib),
    ]

    @pl.when(comes)
    def _():
        for n in range(half, each):
            forward[each + n].wait_recv()

    for f in range(2):
        silu_rows(f, 0, 1)
        silu_rows(f, rows + 3, 1)
    first([(0, rows + 2)])
    send_mid[0].start()
    send_mid[1].start()
    send_mid[2].start()

    lines = (rows + 1) * cols

    def second(half, then):
        def gather(f):
            return jnp.concatenate(
                [mid[half, f, pl.ds(q, rows + 1)].reshape(lines, h1) for q in range(2)], axis=1
            )

        earlier = gather(0)
        both = jnp.concatenate([earlier, gather(1)], axis=0)
        for p in range(2):
            for outer in range(2):
                now = jnp.dot(both, m2[1, half, p, outer], preferred_element_type=F32)
                early = jnp.dot(earlier, m2[0, half, p, outer], preferred_element_type=F32)
                for f in range(2):
                    then(p, outer, f, now[f * lines : (f + 1) * lines] + early)

    def keep(p, outer, f, value):
        acc2[p, outer, f] = value

    def add(p, outer, f, value):
        acc2[p, outer, f] = acc2[p, outer, f] + value

    second(0, keep)
    for copy in send_mid:
        copy.wait_recv()
    second(1, add)

    send_low = [
        remote(low.at[0, f], low.at[1, f], low_send.at[f], low_recv.at[f], sib) for f in range(2)
    ]
    last = 2 * rows + 1
    for f in range(2):
        for p in range(2):
            inner, outer = acc2[p, 0, f], acc2[p, 1, f]
            values = [
                inner[:, :h2] + shifts(outer[:, :h2])[0](),
                inner[:, h2:] + shifts(outer[:, h2:])[1](),
            ]
            for phase in range(2):
                value = silu(values[phase] + bias2)
                for m in range(rows + 1):
                    row = 2 * m + 1 - p
                    part = value[m * cols : (m + 1) * cols]
                    if row == 0:
                        part = jnp.where(has_up, part, 0.0)
                    if row == last:
                        part = jnp.where(has_down, part, 0.0)
                    low[0, f, phase, row] = part.astype(BF16)
        if f == 0:
            send_low[0].start()
        else:
            pl.when(s == 0)(send_low[1].start)

    deep = 2 * rows * cols

    def third(half, p, phase):
        x = jnp.concatenate(
            [
                low[half, f, phase, pl.ds(p + q, 2 * rows)].reshape(deep, h2)
                for f in (0, s)
                for q in range(2)
            ],
            axis=1,
        )
        return [
            jnp.dot(
                x,
                jnp.concatenate([m3[0, half, p, outer], m3[1, half, p, outer]], axis=0),
                preferred_element_type=F32,
            )
            for outer in range(2)
        ]

    for p in range(2):
        for phase in range(2):
            for outer, value in enumerate(third(0, p, phase)):
                acc3[p, phase, outer] = value
    send_low[0].wait_recv()
    pl.when(s == 1)(send_low[1].wait_recv)
    for p in range(2):
        inner, outer = [], []
        for phase in range(2):
            a, b = third(1, p, phase)
            inner.append(acc3[p, phase, 0] + a)
            outer.append(acc3[p, phase, 1] + b)
        values = [
            inner[0][:, :c3] + shifts(outer[1][:, :c3])[0](),
            inner[0][:, c3:] + outer[1][:, c3:],
            inner[1][:, :c3] + outer[0][:, :c3],
            inner[1][:, c3:] + shifts(outer[0][:, c3:])[1](),
        ]
        for n in range(4):
            for m in range(2 * rows):
                stage[p, m, pl.ds(n, cols, stride=4), :] = values[n][m * cols : (m + 1) * cols] + bias3
        for m in range(2 * rows):
            row = 2 * m + p
            out[0, row] = stage[p, m].astype(BF16)

    for n in range(each):
        pair[n].wait_send()
        forward[n].wait_send()
        pl.when(goes)(relay[n].wait_send)
        pl.when(comes)(forward[each + n].wait_send)
    swap.wait_send()
    for c in send_mid:
        c.wait_send()
    send_low[0].wait_send()
    pl.when(s == 0)(send_low[1].wait_send)


def per_device(features, w1, b1, w2, b2, w3, b3):
    count = lax.axis_size("tile")
    _, rows, cols, c1 = features.shape
    c2, c3 = w2.shape[4], w3.shape[4]
    h1, h2 = c1 // 2, c2 // 2
    anywhere = pl.BlockSpec(memory_space=pltpu.HBM)
    vmem = pl.BlockSpec(memory_space=pltpu.VMEM)
    dma = pltpu.SemaphoreType.DMA
    features, b1, b2, b3 = [
        pltpu.with_memory_space_constraint(x, pltpu.HBM) for x in (features, b1, b2, b3)
    ]
    return pl.pallas_call(
        functools.partial(kernel, count),
        out_shape=jax.ShapeDtypeStruct((1, 4 * rows, 4 * cols, c3), BF16),
        in_specs=[anywhere] * 7,
        out_specs=vmem,
        scratch_shapes=[
            pltpu.VMEM((2, rows + 4, cols, c1), BF16),
            pltpu.VMEM((2, (rows + 4) * cols, c1), BF16),
            pltpu.VMEM((c1,), BF16),
            pltpu.VMEM((c2,), BF16),
            pltpu.VMEM((c3,), BF16),
            pltpu.VMEM((3, 3, 3, c1, h1), BF16),
            pltpu.VMEM((2, 3, 3, 3, h1, h2), BF16),
            pltpu.VMEM((2, 3, 3, 3, h2, c3), BF16),
            pltpu.VMEM((2, 2, 2, 2, 2 * h1, 2 * h2), BF16),
            pltpu.VMEM((2, 2, 2, 2, 2 * h2, 2 * c3), BF16),
            pltpu.VMEM((2, 2, rows + 2, cols, h1), BF16),
            pltpu.VMEM((2, 2, 2, 2 * rows + 2, cols, h2), BF16),
            pltpu.VMEM((2, 2, 2, (rows + 1) * cols, 2 * h2), F32),
            pltpu.VMEM((2, 2, 2, 2 * rows * cols, 2 * c3), F32),
            pltpu.VMEM((2, 2 * rows, 4 * cols, c3), F32),
            dma((10,)),
            dma(()),
            dma((4 * PIECES,)),
            dma((4 * PIECES,)),
            dma((4 * PIECES + 1,)),
            dma((4 * PIECES + 1,)),
            dma((3,)),
            dma((3,)),
            dma((2,)),
            dma((2,)),
        ],
        compiler_params=pltpu.CompilerParams(
            collective_id=0, has_side_effects=True, vmem_limit_bytes=52 * 2**20
        ),
    )(features, w1, b1, w2, b2, w3, b3)


def solution(mesh):
    return jax.shard_map(
        per_device,
        mesh=mesh,
        in_specs=(P(("groups", "sect"), "tile", None, None), P(), P(), P(), P(), P(), P()),
        out_specs=P(("groups", "sect"), "tile", None, None),
        check_vma=False,
    )
```
